256 devices in a mesh: dp: 32 (over y, x, core), head: 8 (over z).
Axes of the slice: x: 4, y: 4, z: 8, core: 2. Of those that a mesh axis runs over, the one named last changes fastest.
Arguments:
- queries: bfloat16 [32768, 8192], P(('dp', 'head')), may hold values from -80 to 80
- input_keys: bfloat16 [32768, 1024], P(('dp', 'head')), may hold values from -4 to 4
- input_values: bfloat16 [32768, 1024], P(('dp', 'head')), may hold values from -6 to 6
- output_gradient: bfloat16 [32768, 8192], P(('dp', 'head')), may hold values from -6 to 6
- doc_ids: int32 [32768], P('dp'), may hold values from 0 to 63, as said below
- spill_src: int32 [32], replicated, may hold values from 0 to 31, as said below
- spill_len: int32 [32], replicated, may hold values from 1 to 128, as said below
Outputs:
- attn_out: bfloat16 [32768, 8192], P(('dp', 'head'))
- grad_queries: bfloat16 [32768, 8192], P(('dp', 'head'))
- grad_keys: bfloat16 [32768, 1024], P(('dp', 'head'))
- grad_values: bfloat16 [32768, 1024], P(('dp', 'head'))
The draws below stay inside these ranges and needn't reach their ends.
Inputs may be any that keep to these rules, and one draw needn't show every extreme that they name: `doc_ids`: within each bin of 1024 tokens the document numbers start at 0, never fall and rise by at most one from one token to the next; the last document of every bin holds more than 128 tokens; some bin reaches the largest. `spill_src`: every bin is the source of exactly one bin and never its own source. `spill_len`: the value 128 is taken by some bin in every draw.
All inputs are finite; a program needn't handle non-finite values.
Results may differ from the reference program's by a relative error of at most 0.04.
Values may be sent and summed in bfloat16 or wider, within the bound.
No kernel may reach another device: no remote copies, remote signals or barrier semaphores. Data moves between devices by JAX's collectives and lax.ppermute only.
A program may use at most 192 MiB of HBM per device.

```python
import jax
import jax.numpy as jnp
from jax import lax

QUERY_HEADS = 64
KEY_VALUE_HEADS = 8
HEAD_SIZE = 128
BIN_TOKENS = 1024
TAIL = 128
TOTAL_TOKENS = 32768
N_DP = 32


def shared_keys(key):
    starting_keys = jax.random.normal(jax.random.fold_in(key, 101), (TOTAL_TOKENS, KEY_VALUE_HEADS, HEAD_SIZE), jnp.float32)
    starting_keys = jnp.clip(starting_keys, -4.0, 4.0)
    return starting_keys


def spill_cycle(key):
    return jax.random.permutation(jax.random.fold_in(key, 201), N_DP)


def draw_input_keys(key, part):
    starting_keys = shared_keys(key)
    return starting_keys.reshape(TOTAL_TOKENS, KEY_VALUE_HEADS * HEAD_SIZE).astype(jnp.bfloat16)


def draw_queries(key, part):
    key = jax.random.fold_in(key, 2)
    head_groups = QUERY_HEADS // KEY_VALUE_HEADS
    newest_rows = jnp.clip(jax.random.normal(key, (TOTAL_TOKENS, KEY_VALUE_HEADS, head_groups, HEAD_SIZE), jnp.float32), -4.0, 4.0)
    return newest_rows.reshape(TOTAL_TOKENS, QUERY_HEADS * HEAD_SIZE).astype(jnp.bfloat16)


def draw_doc_ids(key, part):
    key = jax.random.fold_in(key, 4)
    most_docs = BIN_TOKENS // 16
    counts = jax.random.randint(jax.random.fold_in(key, 1), (N_DP,), 1, most_docs + 1)
    fullest = jax.random.randint(jax.random.fold_in(key, 2), (), 0, N_DP)
    counts = counts.at[fullest].set(most_docs)
    bin_keys = jax.random.split(jax.random.fold_in(key, 3), N_DP)
    ranks = jax.vmap(lambda one_key: jax.random.permutation(one_key, BIN_TOKENS - TAIL - 1))(bin_keys)
    boundary = ranks < counts[:, None] - 1
    steps_up = jnp.concatenate([jnp.zeros((N_DP, 1), jnp.int32), boundary.astype(jnp.int32), jnp.zeros((N_DP, TAIL), jnp.int32)], axis=1)
    return jnp.cumsum(steps_up, axis=1).astype(jnp.int32).reshape(TOTAL_TOKENS)


def draw_spill_src(key, part):
    cycle_order = spill_cycle(key)
    following = jnp.roll(cycle_order, -1)
    return jnp.zeros((N_DP,), jnp.int32).at[following].set(cycle_order.astype(jnp.int32))


def draw_spill_len(key, part):
    cycle_order = spill_cycle(key)
    key = jax.random.fold_in(key, 6)
    lengths = jax.random.randint(key, (N_DP,), 1, TAIL + 1)
    return lengths.at[cycle_order[0]].set(TAIL).astype(jnp.int32)


def shard_levels(key, extent, shards, low, largest):
    loudness, own = 1.0, jax.random.fold_in(key, 6)
    for position, shards_of in shards:
        heights = jnp.exp(jax.random.uniform(jax.random.fold_in(own, position), (shards_of,), jnp.float32, low / len(shards), largest / len(shards)))
        loudness = loudness * jnp.repeat(heights, extent[position] // shards_of).reshape([-1 if axis == position else 1 for axis in range(len(extent))])
    return loudness


def centred(stream_key, dims, spread, most, shards=(), kind=jnp.bfloat16):
    result = jax.random.normal(stream_key, dims, jnp.float32) * spread
    if len(shards) > 0:
        result = shard_levels(stream_key, dims, shards, -0.22, 0.18) * result
    return jnp.clip(result, min=-most, max=most).astype(kind)


def setup_inputs(seed: int = 0) -> dict:
    arg_keys = jax.random.split(jax.random.key(seed), 8)
    return {
        "queries": draw_queries(jax.random.fold_in(arg_keys[7], 71), 0),
        "input_keys": draw_input_keys(jax.random.fold_in(arg_keys[7], 71), 0),
        "input_values": centred(arg_keys[2], (TOTAL_TOKENS, KEY_VALUE_HEADS * HEAD_SIZE), 1.0, 6.0, ((0, 256),)),
        "output_gradient": centred(arg_keys[3], (TOTAL_TOKENS, QUERY_HEADS * HEAD_SIZE), 1.0, 6.0, ((0, 256),)),
        "doc_ids": draw_doc_ids(jax.random.fold_in(arg_keys[7], 71), 0),
        "spill_src": draw_spill_src(jax.random.fold_in(arg_keys[7], 71), 0),
        "spill_len": draw_spill_len(jax.random.fold_in(arg_keys[7], 71), 0),
    }


def bin_attention(query_bin, grad_bin, key_list, value_list, key_mask):
    scaling = query_bin.shape[-1] ** -0.5
    scores = jnp.einsum("qhgd,khd->hgqk", query_bin.astype(jnp.float32), key_list.astype(jnp.float32)) * scaling
    scores = jnp.where(key_mask, scores, -1e30)
    highest = jnp.max(scores, axis=-1, keepdims=True)
    chances = jnp.exp(scores - highest)
    chances = chances / jnp.sum(chances, axis=-1, keepdims=True)
    weights = lax.optimization_barrier(chances.astype(jnp.bfloat16))
    output = jnp.einsum("hgqk,khd->qhgd", weights.astype(jnp.float32), value_list.astype(jnp.float32))
    output = lax.optimization_barrier(output.astype(jnp.bfloat16))
    grad_w = jnp.einsum("qhgd,khd->hgqk", grad_bin.astype(jnp.float32), value_list.astype(jnp.float32))
    deltas = jnp.einsum("qhgd,qhgd->hgq", grad_bin.astype(jnp.float32), output.astype(jnp.float32))
    grad_s = lax.optimization_barrier((chances * (grad_w - deltas[..., None]) * scaling).astype(jnp.bfloat16))
    grad_q = jnp.einsum("hgqk,khd->qhgd", grad_s.astype(jnp.float32), key_list.astype(jnp.float32))
    grad_k = jnp.einsum("hgqk,qhgd->khd", grad_s.astype(jnp.float32), query_bin.astype(jnp.float32))
    grad_v = jnp.einsum("hgqk,qhgd->khd", weights.astype(jnp.float32), grad_bin.astype(jnp.float32))
    return output, grad_q.astype(jnp.bfloat16), grad_k, grad_v


def reference(queries, input_keys, input_values, output_gradient, doc_ids, spill_src, spill_len):
    head_groups = QUERY_HEADS // KEY_VALUE_HEADS
    binned_queries = queries.reshape(N_DP, BIN_TOKENS, KEY_VALUE_HEADS, head_groups, HEAD_SIZE)
    gradient_bins = output_gradient.reshape(N_DP, BIN_TOKENS, KEY_VALUE_HEADS, head_groups, HEAD_SIZE)
    binned_keys = input_keys.reshape(N_DP, BIN_TOKENS, KEY_VALUE_HEADS, HEAD_SIZE)
    binned_values = input_values.reshape(N_DP, BIN_TOKENS, KEY_VALUE_HEADS, HEAD_SIZE)
    doc_bins = doc_ids.reshape(N_DP, BIN_TOKENS)
    positions = jnp.arange(BIN_TOKENS, dtype=jnp.int32)
    tail_positions = jnp.arange(TAIL, dtype=jnp.int32)

    def one_bin(bundle):
        query_bin, grad_bin, key_near, value_near, documents, source, spilled = bundle
        key_far = binned_keys[source][BIN_TOKENS - TAIL:]
        value_far = binned_values[source][BIN_TOKENS - TAIL:]
        near_mask = (documents[:, None] == documents[None, :]) & (positions[None, :] <= positions[:, None])
        far_mask = (tail_positions[None, :] >= TAIL - spilled) & (documents[:, None] == 0)
        key_mask = jnp.concatenate([far_mask, near_mask], axis=1)
        key_list = jnp.concatenate([key_far, key_near], axis=0)
        value_list = jnp.concatenate([value_far, value_near], axis=0)
        output, grad_q, grad_k, grad_v = bin_attention(query_bin, grad_bin, key_list, value_list, key_mask)
        return output, grad_q, grad_k[TAIL:], grad_v[TAIL:], grad_k[:TAIL], grad_v[:TAIL]

    results = lax.map(one_bin, (binned_queries, gradient_bins, binned_keys, binned_values, doc_bins, spill_src, spill_len))
    output, grad_q, local_keys, local_values, far_k, far_v = results
    local_keys = local_keys.at[spill_src, BIN_TOKENS - TAIL:].add(far_k)
    local_values = local_values.at[spill_src, BIN_TOKENS - TAIL:].add(far_v)
    return (output.reshape(TOTAL_TOKENS, QUERY_HEADS * HEAD_SIZE),
            grad_q.reshape(TOTAL_TOKENS, QUERY_HEADS * HEAD_SIZE),
            local_keys.astype(jnp.bfloat16).reshape(TOTAL_TOKENS, KEY_VALUE_HEADS * HEAD_SIZE),
            local_values.astype(jnp.bfloat16).reshape(TOTAL_TOKENS, KEY_VALUE_HEADS * HEAD_SIZE))
```

```python
import functools

import jax
import jax.numpy as jnp
from jax import lax
from jax.experimental import pallas as pl
from jax.experimental.pallas import tpu as pltpu
from jax.sharding import PartitionSpec as P

HEAD = 128
GROUP = 8
KV_HEADS = 8
ROWS = 128
WIDE = GROUP * ROWS
TAIL = 128
KEYS = 1024 + TAIL
PAIR = 256
LOG2E = 1.4426950408889634
SCALE = HEAD**-0.5
MASKED = -1e30
F32 = jnp.float32
BF16 = jnp.bfloat16
NT = (((1,), (1,)), ((), ()))
TN = (((0,), (0,)), ((), ()))
CHUNKS = [(0, 128)] + [(128 + 256 * i, 256) for i in range(4)]


def dot(a, b, dims=(((1,), (0,)), ((), ()))):
    return lax.dot_general(a, b, dims, preferred_element_type=F32)


def fold(x, op):
    return op(x.reshape(x.shape[0] // 8, 8, x.shape[1]), axis=0)


def body(bias, q_ref, do_ref, near, far, o_ref, dq_ref, dnear, dfar, s_ref, p_ref, dk_ref, dv_ref):
    keys, values = [far[0]], [far[1]]
    for i in range(4):
        keys.append(near[2 * i : 2 * i + 2, 0].reshape(PAIR, HEAD))
        values.append(near[2 * i : 2 * i + 2, 1].reshape(PAIR, HEAD))
    for pair in range(GROUP // 2):
        cut = [slice((2 * pair + h) * HEAD, (2 * pair + h + 1) * HEAD) for h in range(2)]
        q2 = jnp.concatenate([q_ref[:, at] for at in cut], axis=0)
        do2 = jnp.concatenate([do_ref[:, at] for at in cut], axis=0)
        dot2 = jnp.concatenate([do_ref[:, at].T for at in cut], axis=1)
        high = None
        for c, (at, size) in enumerate(CHUNKS):
            mask = bias[at : at + size]
            s = dot(keys[c], q2, NT) * (SCALE * LOG2E) + jnp.concatenate([mask, mask], axis=1)
            s_ref[pair, at : at + size] = s
            top = fold(s, jnp.max)
            high = top if high is None else jnp.maximum(high, top)
        high = jnp.max(high, axis=0, keepdims=True)
        norm = 0.0
        for c, (at, size) in enumerate(CHUNKS):
            p = jnp.exp2(s_ref[pair, at : at + size] - high)
            s_ref[pair, at : at + size] = p
            norm = norm + fold(p, jnp.sum)
        scale = 1.0 / jnp.sum(norm, axis=0, keepdims=True)
        out = 0.0
        for c, (at, size) in enumerate(CHUNKS):
            w = s_ref[pair, at : at + size] * scale
            w16 = w.astype(BF16)
            p_ref[pair, at : at + size] = w16
            out = out + dot(values[c], w16, TN)
        out = out.astype(BF16)
        for h in range(2):
            o_ref[:, cut[h]] = out[:, h * HEAD : (h + 1) * HEAD].T
        delta = jnp.sum(dot2.astype(F32) * out.astype(F32), axis=0, keepdims=True)
        grad = 0.0
        for c, (at, size) in enumerate(CHUNKS):
            w16 = p_ref[pair, at : at + size]
            ds = (w16.astype(F32) * (dot(values[c], dot2) - delta)).astype(BF16)
            dv = dot(w16, do2)
            dk = dot(ds, q2)
            if pair:
                dv_ref[at : at + size] += dv
                dk_ref[at : at + size] += dk
            else:
                dv_ref[at : at + size] = dv
                dk_ref[at : at + size] = dk
            grad = grad + dot(keys[c], ds, TN)
        grad = (grad * SCALE).astype(BF16)
        for h in range(2):
            dq_ref[:, cut[h]] = grad[:, h * HEAD : (h + 1) * HEAD].T
    dk = (dk_ref[...] * SCALE).astype(BF16)
    dv = dv_ref[...].astype(BF16)
    dfar[0], dfar[1] = dk[:TAIL], dv[:TAIL]
    for i in range(8):
        at = slice(TAIL + i * ROWS, TAIL + (i + 1) * ROWS)
        dnear[i, 0], dnear[i, 1] = dk[at], dv[at]


def attend(bias, queries, grad, near, far):
    wide = pl.BlockSpec((ROWS, WIDE), lambda k: (0, k))
    near_spec = pl.BlockSpec((8, 2, ROWS, HEAD), lambda k: (0, 0, 0, k))
    far_spec = pl.BlockSpec((2, ROWS, HEAD), lambda k: (0, 0, k))
    return pl.pallas_call(
        body,
        grid=(KV_HEADS,),
        in_specs=[pl.BlockSpec((KEYS, ROWS), lambda k: (0, 0)), wide, wide, near_spec, far_spec],
        out_specs=[wide, wide, near_spec, far_spec],
        out_shape=[jax.ShapeDtypeStruct(a.shape, BF16) for a in (queries, grad, near, far)],
        scratch_shapes=[
            pltpu.VMEM((GROUP // 2, KEYS, PAIR), F32),
            pltpu.VMEM((GROUP // 2, KEYS, PAIR), BF16),
            pltpu.VMEM((KEYS, HEAD), F32),
            pltpu.VMEM((KEYS, HEAD), F32),
        ],
        compiler_params=pltpu.CompilerParams(vmem_limit_bytes=48 * 2**20),
        cost_estimate=pl.CostEstimate(
            flops=6 * 2 * HEAD * KEYS * WIDE * KV_HEADS,
            bytes_accessed=18 * 2**20,
            transcendentals=KEYS * WIDE * KV_HEADS,
        ),
    )(bias, queries, grad, near, far)


def split(block):
    return block.reshape(2, 16, 8, 8, HEAD).transpose(0, 1, 3, 2, 4).reshape(256, 8, HEAD)


def join(pieces):
    return pieces.reshape(2, 16, 8, 8, HEAD).transpose(0, 1, 3, 2, 4).reshape(2, TAIL, 1024)


def exchange(pieces):
    return lax.all_to_all(pieces, ("dp", "head"), split_axis=0, concat_axis=0, tiled=True)


def per_device(queries, input_keys, input_values, output_gradient, doc_ids, spill_src, spill_len):
    rank, z = lax.axis_index("dp"), lax.axis_index("head")
    ids = jnp.arange(32, dtype=jnp.int32)
    kv = jnp.stack([input_keys, input_values])
    near = lax.all_gather(kv, "head", axis=0)

    pieces = exchange(split(kv)).reshape(32, 8, 8 * HEAD)[:, 7]
    wanted = (spill_src[:, None] == ids[None, :]).astype(BF16)
    pieces = jnp.dot(wanted, pieces, preferred_element_type=F32).astype(BF16)
    pieces = jnp.broadcast_to(pieces.reshape(32, 1, 8, HEAD), (32, 8, 8, HEAD)).reshape(256, 8, HEAD)
    far = join(exchange(pieces))

    place = jnp.arange(1024, dtype=jnp.int32)
    row_at = z * ROWS + jnp.arange(ROWS, dtype=jnp.int32)
    row_docs = lax.dynamic_slice_in_dim(doc_ids, z * ROWS, ROWS)
    near_seen = (doc_ids[:, None] == row_docs[None, :]) & (place[:, None] <= row_at[None, :])
    far_seen = (place[:TAIL, None] >= TAIL - spill_len[rank]) & (row_docs[None, :] == 0)
    seen = jnp.concatenate([far_seen, near_seen], axis=0)
    bias = jnp.where(seen, 0.0, MASKED).astype(F32)

    out, dq, dnear, dfar = attend(bias, queries, output_gradient, near, far)

    home = lax.psum_scatter(dnear, "head", scatter_dimension=0)
    pieces = exchange(split(dfar)).reshape(32, 8, 8 * HEAD)
    pieces = jnp.sum(pieces.astype(F32), axis=1).astype(BF16)
    pieces = jnp.dot(wanted.T, pieces, preferred_element_type=F32).astype(BF16)
    pieces = jnp.broadcast_to(pieces.reshape(32, 1, 8, HEAD), (32, 8, 8, HEAD)).reshape(256, 8, HEAD)
    returned = jnp.where(z == 7, join(exchange(pieces)).astype(F32), 0.0)
    total = (home.astype(F32) + returned).astype(BF16)
    return out, dq, total[0], total[1]


def solution(mesh):
    rows = P(("dp", "head"), None)
    return jax.shard_map(
        per_device,
        mesh=mesh,
        in_specs=(rows, rows, rows, rows, P("dp"), P(), P()),
        out_specs=(rows, rows, rows, rows),
        check_vma=False,
    )
```

```python
import functools

import jax
import jax.numpy as jnp
from jax import lax
from jax.experimental import pallas as pl
from jax.experimental.pallas import tpu as pltpu
from jax.sharding import PartitionSpec as P

HEAD = 128
GROUP = 8
KV_HEADS = 8
ROWS = 128
WIDE = GROUP * ROWS
TAIL = 128
PAIR = 256
LOG2E = 1.4426950408889634
SCALE = HEAD**-0.5
MASKED = -1e30
F32 = jnp.float32
BF16 = jnp.bfloat16
NT = (((1,), (1,)), ((), ()))
TN = (((0,), (0,)), ((), ()))
BLOCK = 512
VMEM = 60 * 2**20


def dot(a, b, dims=(((1,), (0,)), ((), ()))):
    return lax.dot_general(a, b, dims, preferred_element_type=F32)


def fold(x, op):
    return op(x.reshape(x.shape[0] // 8, 8, x.shape[1]), axis=0)


def heads(ref):
    return jnp.concatenate([ref[:, g * HEAD : (g + 1) * HEAD] for g in range(GROUP)], axis=0)


SLICES = [slice(at, at + PAIR) for at in range(0, WIDE, PAIR)]


def stagger(*stages):
    for step in range(len(SLICES) + len(stages) - 1):
        for late, stage in enumerate(stages):
            if 0 <= step - late < len(SLICES):
                stage(SLICES[step - late])


def score(keys, q2, mask):
    return dot(keys, q2, NT) * (SCALE * LOG2E) + jnp.concatenate([mask, mask], axis=1)


def absorb(keys, values, mask, qs, stat, acc, s_ref, p_ref):
    size = keys.shape[0]
    kept = {}

    def scores(at):
        s = score(keys, qs[at], mask)
        s_ref[:size, at] = s
        top = jnp.max(fold(s, jnp.max), axis=0, keepdims=True)
        kept[at.start] = jnp.maximum(stat[0, 0:1, at], top)

    def weights(at):
        high = kept[at.start]
        p = jnp.exp2(s_ref[:size, at] - high)
        p_ref[:size, at] = p.astype(BF16)
        alpha = jnp.exp2(stat[0, 0:1, at] - high)
        stat[0, 0:1, at] = high
        stat[0, 1:2, at] = stat[0, 1:2, at] * alpha + jnp.sum(fold(p, jnp.sum), axis=0, keepdims=True)
        kept[at.start] = alpha

    def mix(at):
        acc[0, :, at] = acc[0, :, at] * kept[at.start] + dot(values, p_ref[:size, at], TN)

    stagger(scores, weights, mix)


def spread(keys, values, mask, qs, dos, stat, dq, s_ref, d_ref, p_ref, ds_ref):
    size = keys.shape[0]
    sums = [0.0, 0.0]

    def scores(at):
        s_ref[:size, at] = score(keys, qs[at], mask) - stat[0, 0:1, at]
        d_ref[:size, at] = dot(values, dos[at], NT) - stat[0, 1:2, at]

    def weights(at):
        p = jnp.exp2(s_ref[:size, at])
        p_ref[:size, at] = p.astype(BF16)
        ds_ref[:size, at] = (p * d_ref[:size, at]).astype(BF16)

    def mix(at):
        sums[0] = sums[0] + dot(ds_ref[:size, at], qs[at])
        sums[1] = sums[1] + dot(p_ref[:size, at], dos[at])
        dq[0, :, at] += dot(keys, ds_ref[:size, at], TN)

    stagger(scores, weights, mix)
    return (sums[0] * SCALE).astype(BF16), sums[1].astype(BF16)


def blocks(span, near, bias, work):
    @pl.loop(span[0], span[1])
    def _(j):
        part = pl.ds(BLOCK // ROWS * j, BLOCK // ROWS)
        keys = near[part, 0].reshape(BLOCK, HEAD)
        values = near[part, 1].reshape(BLOCK, HEAD)
        work(part, keys, values, bias[pl.ds(pl.multiple_of(j * BLOCK, BLOCK), BLOCK)])


def near_fwd_body(span, bias, q_ref, near, stat, acc, qs, s_ref, p_ref):
    qs[...] = heads(q_ref)
    stat[0, 0:1] = jnp.full((1, WIDE), MASKED, F32)
    stat[0, 1:2] = jnp.zeros((1, WIDE), F32)
    acc[...] = jnp.zeros_like(acc)

    def work(part, keys, values, mask):
        absorb(keys, values, mask, qs, stat, acc, s_ref, p_ref)

    blocks(span, near, bias, work)


def tail(far):
    return far[:, 0].reshape(TAIL, HEAD), far[:, 1].reshape(TAIL, HEAD)


def far_body(
    flag, bias, q_ref, do_ref, far, stat_in, acc_in, o_ref, stat_out, dq, dfar, qs, dos, stat, acc, s_ref, d_ref, p_ref, ds_ref
):
    stat[...] = stat_in[...]
    acc[...] = acc_in[...]
    dq[...] = jnp.zeros_like(dq)

    @pl.when(flag[0] > 0)
    def _():
        qs[...] = heads(q_ref)
        dos[...] = heads(do_ref)
        absorb(*tail(far), bias[...], qs, stat, acc, s_ref, p_ref)

    norm = stat[0, 1:2]
    out = (acc[0] * (1.0 / norm)).astype(BF16)
    stat_out[0, 0:1] = stat[0, 0:1] + jnp.log2(norm)
    for g in range(GROUP):
        at = slice(g * HEAD, (g + 1) * HEAD)
        o_ref[:, at] = out[:, at].T
        prod = do_ref[:, at].T.astype(F32) * out[:, at].astype(F32)
        stat_out[0, 1:2, at] = jnp.sum(prod, axis=0, keepdims=True)

    @pl.when(flag[0] > 0)
    def _():
        dk, dv = spread(*tail(far), bias[...], qs, dos, stat_out, dq, s_ref, d_ref, p_ref, ds_ref)
        dfar[:, 0] = dk.reshape(8, 16, HEAD)
        dfar[:, 1] = dv.reshape(8, 16, HEAD)

    @pl.when(flag[0] == 0)
    def _():
        dfar[...] = jnp.zeros_like(dfar)


def near_bwd_body(span, bias, q_ref, do_ref, near, stat, dq_in, *refs):
    dq_ref, dnear, qs, dos, dq, s_ref, d_ref, p_ref, ds_ref = refs[-9:]
    qs[...] = heads(q_ref)
    dos[...] = heads(do_ref)
    dq[...] = dq_in[...]
    dnear[...] = jnp.zeros_like(dnear)

    def work(part, keys, values, mask):
        dk, dv = spread(keys, values, mask, qs, dos, stat, dq, s_ref, d_ref, p_ref, ds_ref)
        dnear[part, 0] = dk.reshape(BLOCK // ROWS, ROWS, HEAD)
        dnear[part, 1] = dv.reshape(BLOCK // ROWS, ROWS, HEAD)

    blocks(span, near, bias, work)
    for g in range(GROUP):
        at = slice(g * HEAD, (g + 1) * HEAD)
        dq_ref[:, at] = (dq[0, :, at] * SCALE).astype(BF16).T


def shape(dims, dtype=BF16):
    return jax.ShapeDtypeStruct(dims, dtype)


STAT = shape((KV_HEADS, 2, WIDE), F32)
ACC = shape((KV_HEADS, HEAD, WIDE), F32)
TALL = shape((WIDE, HEAD))


def spec(a, skip=0):
    if len(a.shape) == 2:
        return pl.BlockSpec((ROWS, WIDE), lambda k: (0, k + skip))
    if len(a.shape) == 4:
        return pl.BlockSpec(a.shape[:3] + (HEAD,), lambda k: (0, 0, 0, k + skip))
    return pl.BlockSpec((1,) + a.shape[1:], lambda k: (k + skip, 0, 0))


def call(body, scalars, bias, args, outs, scratch, keys, products, skip=0, count=KV_HEADS, onto=()):
    size = keys * WIDE * count
    return pl.pallas_call(
        body,
        grid=(count,),
        in_specs=[pl.BlockSpec(memory_space=pltpu.SMEM), pl.BlockSpec(bias.shape, lambda k: (0, 0))]
        + [spec(a, skip) for a in args]
        + [pl.BlockSpec(memory_space=pl.ANY) for a in onto],
        out_specs=[spec(a, skip) for a in outs],
        out_shape=outs,
        scratch_shapes=[pltpu.VMEM(a.shape, a.dtype) for a in scratch],
        input_output_aliases={2 + len(args) + i: i for i in range(len(onto))},
        compiler_params=pltpu.CompilerParams(vmem_limit_bytes=VMEM),
        cost_estimate=pl.CostEstimate(
            flops=4 * products * HEAD * size, bytes_accessed=16 * 2**20, transcendentals=size
        ),
    )(scalars, bias, *args, *onto)


ONE_STAT = shape((1, 2, WIDE), F32)
ONE_ACC = shape((1, HEAD, WIDE), F32)


def slabs(keys):
    return [shape((keys, WIDE), F32), shape((keys, WIDE), F32), shape((keys, WIDE)), shape((keys, WIDE))]


def near_fwd(span, bias, q, near):
    scratch = [TALL, shape((BLOCK, WIDE), F32), shape((BLOCK, WIDE))]
    return call(near_fwd_body, span, bias, [q, near], [STAT, ACC], scratch, 1024, 2)


def far_both(flag, bias, q, grad, far, stat, acc):
    outs = [shape(q.shape), STAT, ACC, shape(far.shape)]
    scratch = [TALL, TALL, ONE_STAT, ONE_ACC, *slabs(TAIL)]
    return call(far_body, flag, bias, [q, grad, far, stat, acc], outs, scratch, TAIL, 12)


def near_bwd(span, bias, q, grad, near, stat, dq, skip, onto=()):
    outs = [shape(q.shape), shape(near.shape)]
    scratch = [TALL, TALL, ONE_ACC, *slabs(BLOCK)]
    args = [q, grad, near, stat, dq]
    return call(near_bwd_body, span, bias, args, outs, scratch, 1024, 5, skip, KV_HEADS // 2, onto)


def split(block):
    rows = block.shape[1] // 8
    return block.reshape(2, rows, 8, 8, HEAD).transpose(0, 1, 3, 2, 4).reshape(16 * rows, 8, HEAD)


def join(pieces):
    rows = pieces.shape[0] // 16
    return pieces.reshape(2, rows, 8, 8, HEAD).transpose(0, 1, 3, 2, 4).reshape(2, rows * 8, 1024)


def swap(pieces, axis):
    return lax.all_to_all(pieces, axis, split_axis=0, concat_axis=0, tiled=True)


def route(block, choose):
    pieces = swap(split(block), "dp").reshape(32, 8 * HEAD)
    pieces = jnp.dot(choose, pieces, preferred_element_type=F32).astype(BF16)
    return join(swap(pieces.reshape(32, 8, HEAD), "dp"))


def scatter_last(kv, z):
    half = lax.ppermute(kv[:, :64], "head", [(7, 3)])
    mine = jnp.where(z == 7, kv[:, 64:], half)
    send = jnp.where(z == 7, mine[:, :32], half[:, :32])
    quarter = lax.ppermute(send, "head", [(7, 5), (3, 1)])
    send = jnp.where(z % 4 == 3, mine[:, 32:48], quarter[:, :16])
    eighth = lax.ppermute(send, "head", [(7, 6), (5, 4), (3, 2), (1, 0)])
    return jnp.where(z % 2 == 0, eighth, jnp.where(z % 4 == 1, quarter[:, 16:], mine[:, 48:]))


def collect_last(piece):
    two = lax.ppermute(piece, "head", [(i, i + 1) for i in (0, 2, 4, 6)])
    two = jnp.concatenate([two, piece], axis=1)
    four = lax.ppermute(two, "head", [(1, 3), (5, 7)])
    four = jnp.concatenate([four, two], axis=1)
    eight = lax.ppermute(four, "head", [(3, 7)])
    return jnp.concatenate([eight, four], axis=1)


def per_device(queries, input_keys, input_values, output_gradient, doc_ids, spill_src, spill_len):
    rank, z = lax.axis_index("dp"), lax.axis_index("head")
    ids = jnp.arange(32, dtype=jnp.int32)
    kv = jnp.stack([input_keys, input_values])
    near = lax.all_gather(kv, "head", axis=0)

    wanted = (spill_src[:, None] == ids[None, :]).astype(BF16)
    piece = route(scatter_last(kv, z), wanted)
    near, piece = lax.optimization_barrier((near, piece))
    far = swap(jnp.broadcast_to(piece[None], (8, 2, 16, 1024)), "head")

    place = jnp.arange(1024, dtype=jnp.int32)
    row_at = z * ROWS + jnp.arange(ROWS, dtype=jnp.int32)
    row_docs = lax.dynamic_slice_in_dim(doc_ids, z * ROWS, ROWS)
    near_seen = (doc_ids[:, None] == row_docs[None, :]) & (place[:, None] <= row_at[None, :])
    far_seen = (place[:TAIL, None] >= TAIL - spill_len[rank]) & (row_docs[None, :] == 0)
    near_bias = jnp.where(near_seen, 0.0, MASKED).astype(F32)
    far_bias = jnp.where(far_seen, 0.0, MASKED).astype(F32)
    closing = doc_ids.reshape(8, ROWS)[:, ROWS - 1]
    begin = jnp.sum((closing < row_docs[0]).astype(jnp.int32))
    span = jnp.stack([begin // 4, z // 4 + 1])
    flag = (row_docs[:1] == 0).astype(jnp.int32)

    stat, acc = near_fwd(span, near_bias, queries, near)
    out, stat, dq, dfar = far_both(flag, far_bias, queries, output_gradient, far, stat, acc)
    parts = swap(dfar, "head")
    args = (span, near_bias, queries, output_gradient, near, stat, dq)
    half = near_bwd(*args, 0)
    half, parts = lax.optimization_barrier((half, parts))
    dq, dnear = near_bwd(*args, KV_HEADS // 2, half)

    home = lax.psum_scatter(dnear, "head", scatter_dimension=0)
    piece = jnp.sum(parts.astype(F32), axis=0).astype(BF16)
    returned = collect_last(route(piece, wanted.T))
    returned = jnp.where(z == 7, returned.astype(F32), 0.0)
    total = (home.astype(F32) + returned).astype(BF16)
    return out, dq, total[0], total[1]


def solution(mesh):
    rows = P(("dp", "head"), None)
    return jax.shard_map(
        per_device,
        mesh=mesh,
        in_specs=(rows, rows, rows, rows, P("dp"), P(), P()),
        out_specs=(rows, rows, rows, rows),
        check_vma=False,
    )
```

```python
import functools

import jax
import jax.numpy as jnp
from jax import lax
from jax.experimental import pallas as pl
from jax.experimental.pallas import tpu as pltpu
from jax.sharding import PartitionSpec as P

HEAD = 128
GROUP = 8
KV_HEADS = 8
ROWS = 128
WIDE = GROUP * ROWS
TAIL = 128
PAIR = 256
LOG2E = 1.4426950408889634
SCALE = HEAD**-0.5
MASKED = -1e30
F32 = jnp.float32
BF16 = jnp.bfloat16
NT = (((1,), (1,)), ((), ()))
TN = (((0,), (0,)), ((), ()))
BLOCK = 512
PACK = 2
VMEM = 60 * 2**20


def dot(a, b, dims=(((1,), (0,)), ((), ()))):
    return lax.dot_general(a, b, dims, preferred_element_type=F32)


def fold(x, op):
    return op(x.reshape(x.shape[0] // 8, 8, x.shape[1]), axis=0)


def heads(ref):
    return jnp.concatenate([ref[:, g * HEAD : (g + 1) * HEAD] for g in range(PACK * GROUP)], axis=0)


SLICES = [(at // WIDE, slice(at % WIDE, at % WIDE + PAIR), slice(at, at + PAIR)) for at in range(0, PACK * WIDE, PAIR)]


def stagger(*stages):
    for step in range(len(SLICES) + len(stages) - 1):
        for late, stage in enumerate(stages):
            if 0 <= step - late < len(SLICES):
                stage(*SLICES[step - late])


def score(keys, q2, mask):
    return dot(keys, q2, NT) * (SCALE * LOG2E) + jnp.concatenate([mask, mask], axis=1)


def absorb(keys, values, mask, qs, stat, acc, s_ref, p_ref):
    size = keys[0].shape[0]
    kept = {}

    def scores(h, at, to):
        s = score(keys[h], qs[to], mask)
        s_ref[:size, to] = s
        top = jnp.max(fold(s, jnp.max), axis=0, keepdims=True)
        kept[to.start] = jnp.maximum(stat[h, 0:1, at], top)

    def weights(h, at, to):
        high = kept[to.start]
        p = jnp.exp2(s_ref[:size, to] - high)
        p_ref[:size, to] = p.astype(BF16)
        alpha = jnp.exp2(stat[h, 0:1, at] - high)
        stat[h, 0:1, at] = high
        stat[h, 1:2, at] = stat[h, 1:2, at] * alpha + jnp.sum(fold(p, jnp.sum), axis=0, keepdims=True)
        kept[to.start] = alpha

    def mix(h, at, to):
        acc[h, :, at] = acc[h, :, at] * kept[to.start] + dot(values[h], p_ref[:size, to], TN)

    stagger(scores, weights, mix)


def spread(keys, values, mask, qs, dos, stat, dq, s_ref, d_ref, p_ref, ds_ref):
    size = keys[0].shape[0]
    dk, dv = [0.0] * PACK, [0.0] * PACK

    def scores(h, at, to):
        s_ref[:size, to] = score(keys[h], qs[to], mask) - stat[h, 0:1, at]
        d_ref[:size, to] = dot(values[h], dos[to], NT) - stat[h, 1:2, at]

    def weights(h, at, to):
        p = jnp.exp2(s_ref[:size, to])
        p_ref[:size, to] = p.astype(BF16)
        ds_ref[:size, to] = (p * d_ref[:size, to]).astype(BF16)

    def mix(h, at, to):
        dk[h] = dk[h] + dot(ds_ref[:size, to], qs[to])
        dv[h] = dv[h] + dot(p_ref[:size, to], dos[to])
        dq[h, :, at] += dot(keys[h], ds_ref[:size, to], TN)

    stagger(scores, weights, mix)
    return [(x * SCALE).astype(BF16) for x in dk], [x.astype(BF16) for x in dv]


def lane(h):
    return slice(h * HEAD, (h + 1) * HEAD)


def blocks(span, near, bias, work):
    @pl.loop(span[0], span[1])
    def _(j):
        part = pl.ds(BLOCK // ROWS * j, BLOCK // ROWS)
        keys = [near[part, 0, :, lane(h)].reshape(BLOCK, HEAD) for h in range(PACK)]
        values = [near[part, 1, :, lane(h)].reshape(BLOCK, HEAD) for h in range(PACK)]
        work(part, keys, values, bias[pl.ds(pl.multiple_of(j * BLOCK, BLOCK), BLOCK)])


def near_fwd_body(span, bias, q_ref, near, stat, acc, qs, s_ref, p_ref):
    qs[...] = heads(q_ref)
    stat[:, 0:1] = jnp.full((PACK, 1, WIDE), MASKED, F32)
    stat[:, 1:2] = jnp.zeros((PACK, 1, WIDE), F32)
    acc[...] = jnp.zeros_like(acc)

    def work(part, keys, values, mask):
        absorb(keys, values, mask, qs, stat, acc, s_ref, p_ref)

    blocks(span, near, bias, work)


def tail(far, which):
    return [far[:, which, :, lane(h)].reshape(TAIL, HEAD) for h in range(PACK)]


def far_body(
    flag, bias, q_ref, do_ref, far, stat_in, acc_in, o_ref, stat_out, dq, dfar, qs, dos, stat, acc, s_ref, d_ref, p_ref, ds_ref
):
    stat[...] = stat_in[...]
    acc[...] = acc_in[...]
    dq[...] = jnp.zeros_like(dq)

    @pl.when(flag[0] > 0)
    def _():
        qs[...] = heads(q_ref)
        dos[...] = heads(do_ref)
        absorb(tail(far, 0), tail(far, 1), bias[...], qs, stat, acc, s_ref, p_ref)

    for h in range(PACK):
        norm = stat[h, 1:2]
        out = (acc[h] * (1.0 / norm)).astype(BF16)
        stat_out[h, 0:1] = stat[h, 0:1] + jnp.log2(norm)
        for g in range(GROUP):
            at, to = lane(g), lane(h * GROUP + g)
            o_ref[:, to] = out[:, at].T
            prod = do_ref[:, to].T.astype(F32) * out[:, at].astype(F32)
            stat_out[h, 1:2, at] = jnp.sum(prod, axis=0, keepdims=True)

    @pl.when(flag[0] > 0)
    def _():
        dk, dv = spread(
            tail(far, 0), tail(far, 1), bias[...], qs, dos, stat_out, dq, s_ref, d_ref, p_ref, ds_ref
        )
        for h in range(PACK):
            dfar[:, 0, :, lane(h)] = dk[h].reshape(8, 16, HEAD)
            dfar[:, 1, :, lane(h)] = dv[h].reshape(8, 16, HEAD)

    @pl.when(flag[0] == 0)
    def _():
        dfar[...] = jnp.zeros_like(dfar)


def near_bwd_body(span, bias, q_ref, do_ref, near, stat, dq_in, dq_ref, dnear, qs, dos, dq, s_ref, d_ref, p_ref, ds_ref):
    qs[...] = heads(q_ref)
    dos[...] = heads(do_ref)
    dq[...] = dq_in[...]
    dnear[...] = jnp.zeros_like(dnear)

    def work(part, keys, values, mask):
        dk, dv = spread(keys, values, mask, qs, dos, stat, dq, s_ref, d_ref, p_ref, ds_ref)
        for h in range(PACK):
            dnear[part, 0, :, lane(h)] = dk[h].reshape(BLOCK // ROWS, ROWS, HEAD)
            dnear[part, 1, :, lane(h)] = dv[h].reshape(BLOCK // ROWS, ROWS, HEAD)

    blocks(span, near, bias, work)
    for h in range(PACK):
        for g in range(GROUP):
            dq_ref[:, lane(h * GROUP + g)] = (dq[h, :, lane(g)] * SCALE).astype(BF16).T


def shape(dims, dtype=BF16):
    return jax.ShapeDtypeStruct(dims, dtype)


STAT = shape((KV_HEADS, 2, WIDE), F32)
ACC = shape((KV_HEADS, HEAD, WIDE), F32)
TALL = shape((PACK * WIDE, HEAD))


def spec(a):
    if len(a.shape) == 2:
        return pl.BlockSpec((ROWS, PACK * WIDE), lambda k: (0, k))
    if len(a.shape) == 4:
        return pl.BlockSpec(a.shape[:3] + (PACK * HEAD,), lambda k: (0, 0, 0, k))
    return pl.BlockSpec((PACK,) + a.shape[1:], lambda k: (k, 0, 0))


def call(body, scalars, bias, args, outs, scratch, keys, products):
    size = keys * WIDE * KV_HEADS
    return pl.pallas_call(
        body,
        grid=(KV_HEADS // PACK,),
        in_specs=[pl.BlockSpec(memory_space=pltpu.SMEM), pl.BlockSpec(bias.shape, lambda k: (0, 0))]
        + [spec(a) for a in args],
        out_specs=[spec(a) for a in outs],
        out_shape=outs,
        scratch_shapes=[pltpu.VMEM(a.shape, a.dtype) for a in scratch],
        compiler_params=pltpu.CompilerParams(vmem_limit_bytes=VMEM),
        cost_estimate=pl.CostEstimate(
            flops=4 * products * HEAD * size, bytes_accessed=16 * 2**20, transcendentals=size
        ),
    )(scalars, bias, *args)


ONE_STAT = shape((PACK, 2, WIDE), F32)
ONE_ACC = shape((PACK, HEAD, WIDE), F32)


def slabs(keys):
    wide = (keys, PACK * WIDE)
    return [shape(wide, F32), shape(wide, F32), shape(wide), shape(wide)]


def near_fwd(span, bias, q, near):
    scratch = [TALL, slabs(BLOCK)[0], slabs(BLOCK)[2]]
    return call(near_fwd_body, span, bias, [q, near], [STAT, ACC], scratch, 1024, 2)


def far_both(flag, bias, q, grad, far, stat, acc):
    outs = [shape(q.shape), STAT, ACC, shape(far.shape)]
    scratch = [TALL, TALL, ONE_STAT, ONE_ACC, *slabs(TAIL)]
    return call(far_body, flag, bias, [q, grad, far, stat, acc], outs, scratch, TAIL, 12)


def near_bwd(span, bias, q, grad, near, stat, dq):
    outs = [shape(q.shape), shape(near.shape)]
    scratch = [TALL, TALL, ONE_ACC, *slabs(BLOCK)]
    args = [q, grad, near, stat, dq]
    return call(near_bwd_body, span, bias, args, outs, scratch, 1024, 5)


def split(block):
    rows = block.shape[1] // 8
    return block.reshape(2, rows, 8, 8, HEAD).transpose(0, 1, 3, 2, 4).reshape(16 * rows, 8, HEAD)


def join(pieces):
    rows = pieces.shape[0] // 16
    return pieces.reshape(2, rows, 8, 8, HEAD).transpose(0, 1, 3, 2, 4).reshape(2, rows * 8, 1024)


def swap(pieces, axis):
    return lax.all_to_all(pieces, axis, split_axis=0, concat_axis=0, tiled=True)


def route(block, choose):
    pieces = swap(split(block), "dp").reshape(32, 8 * HEAD)
    pieces = jnp.dot(choose, pieces, preferred_element_type=F32).astype(BF16)
    return join(swap(pieces.reshape(32, 8, HEAD), "dp"))


def scatter_last(kv, z):
    half = lax.ppermute(kv[:, :64], "head", [(7, 3)])
    mine = jnp.where(z == 7, kv[:, 64:], half)
    send = jnp.where(z == 7, mine[:, :32], half[:, :32])
    quarter = lax.ppermute(send, "head", [(7, 5), (3, 1)])
    send = jnp.where(z % 4 == 3, mine[:, 32:48], quarter[:, :16])
    eighth = lax.ppermute(send, "head", [(7, 6), (5, 4), (3, 2), (1, 0)])
    return jnp.where(z % 2 == 0, eighth, jnp.where(z % 4 == 1, quarter[:, 16:], mine[:, 48:]))


def collect_last(piece):
    two = lax.ppermute(piece, "head", [(i, i + 1) for i in (0, 2, 4, 6)])
    two = jnp.concatenate([two, piece], axis=1)
    four = lax.ppermute(two, "head", [(1, 3), (5, 7)])
    four = jnp.concatenate([four, two], axis=1)
    eight = lax.ppermute(four, "head", [(3, 7)])
    return jnp.concatenate([eight, four], axis=1)


def per_device(queries, input_keys, input_values, output_gradient, doc_ids, spill_src, spill_len):
    rank, z = lax.axis_index("dp"), lax.axis_index("head")
    ids = jnp.arange(32, dtype=jnp.int32)
    kv = jnp.stack([input_keys, input_values])
    near = lax.all_gather(kv, "head", axis=0)

    wanted = (spill_src[:, None] == ids[None, :]).astype(BF16)
    piece = route(scatter_last(kv, z), wanted)
    near, piece = lax.optimization_barrier((near, piece))
    far = swap(jnp.broadcast_to(piece[None], (8, 2, 16, 1024)), "head")

    place = jnp.arange(1024, dtype=jnp.int32)
    row_at = z * ROWS + jnp.arange(ROWS, dtype=jnp.int32)
    row_docs = lax.dynamic_slice_in_dim(doc_ids, z * ROWS, ROWS)
    near_seen = (doc_ids[:, None] == row_docs[None, :]) & (place[:, None] <= row_at[None, :])
    far_seen = (place[:TAIL, None] >= TAIL - spill_len[rank]) & (row_docs[None, :] == 0)
    near_bias = jnp.where(near_seen, 0.0, MASKED).astype(F32)
    far_bias = jnp.where(far_seen, 0.0, MASKED).astype(F32)
    closing = doc_ids.reshape(8, ROWS)[:, ROWS - 1]
    begin = jnp.sum((closing < row_docs[0]).astype(jnp.int32))
    span = jnp.stack([begin // 4, z // 4 + 1])
    flag = (row_docs[:1] == 0).astype(jnp.int32)

    stat, acc = near_fwd(span, near_bias, queries, near)
    out, stat, dq, dfar = far_both(flag, far_bias, queries, output_gradient, far, stat, acc)
    parts = swap(dfar, "head")
    args = (span, near_bias, queries, output_gradient, near, stat, dq)
    dq, dnear = near_bwd(*args)
    dnear, parts = lax.optimization_barrier((dnear, parts))

    home = lax.psum_scatter(dnear, "head", scatter_dimension=0)
    piece = jnp.sum(parts.astype(F32), axis=0).astype(BF16)
    returned = collect_last(route(piece, wanted.T))
    totals = [
        (home[i].astype(F32) + jnp.where(z == 7, returned[i].astype(F32), 0.0)).astype(BF16) for i in range(2)
    ]
    return out, dq, *totals


def solution(mesh):
    rows = P(("dp", "head"), None)
    return jax.shard_map(
        per_device,
        mesh=mesh,
        in_specs=(rows, rows, rows, rows, P("dp"), P(), P()),
        out_specs=(rows, rows, rows, rows),
        check_vma=False,
    )
```

```python
import functools

import jax
import jax.numpy as jnp
from jax import lax
from jax.experimental import pallas as pl
from jax.experimental.pallas import tpu as pltpu
from jax.sharding import PartitionSpec as P

HEAD = 128
GROUP = 8
KV_HEADS = 8
ROWS = 128
WIDE = GROUP * ROWS
TAIL = 128
PAIR = 256
LOG2E = 1.4426950408889634
SCALE = HEAD**-0.5
MASKED = -1e30
F32 = jnp.float32
BF16 = jnp.bfloat16
NT = (((1,), (1,)), ((), ()))
TN = (((0,), (0,)), ((), ()))
KEYS = 1024
PACK = 2
VMEM = 60 * 2**20


def dot(a, b, dims=(((1,), (0,)), ((), ()))):
    return lax.dot_general(a, b, dims, preferred_element_type=F32)


def fold(x, op):
    return op(x.reshape(x.shape[0] // 8, 8, x.shape[1]), axis=0)


def heads(ref):
    return jnp.concatenate([ref[:, g * HEAD : (g + 1) * HEAD] for g in range(PACK * GROUP)], axis=0)


SLICES = [(at // WIDE, slice(at % WIDE, at % WIDE + PAIR), slice(at, at + PAIR)) for at in range(0, PACK * WIDE, PAIR)]


def stagger(*stages):
    for step in range(len(SLICES) + len(stages) - 1):
        for late, stage in enumerate(stages):
            if 0 <= step - late < len(SLICES):
                stage(*SLICES[step - late])


def score(keys, q2, mask):
    return dot(keys, q2, NT) * (SCALE * LOG2E) + jnp.concatenate([mask, mask], axis=1)


def absorb(keys, values, mask, qs, stat, acc, s_ref, p_ref):
    size = keys[0].shape[0]
    kept = {}

    def scores(h, at, to):
        s = score(keys[h], qs[to], mask)
        s_ref[:size, to] = s
        top = jnp.max(fold(s, jnp.max), axis=0, keepdims=True)
        kept[to.start] = jnp.maximum(stat[h, 0:1, at], top)

    def weights(h, at, to):
        high = kept[to.start]
        p = jnp.exp2(s_ref[:size, to] - high)
        p_ref[:size, to] = p.astype(BF16)
        alpha = jnp.exp2(stat[h, 0:1, at] - high)
        stat[h, 0:1, at] = high
        stat[h, 1:2, at] = stat[h, 1:2, at] * alpha + jnp.sum(fold(p, jnp.sum), axis=0, keepdims=True)
        kept[to.start] = alpha

    def mix(h, at, to):
        acc[h, :, at] = acc[h, :, at] * kept[to.start] + dot(values[h], p_ref[:size, to], TN)

    stagger(scores, weights, mix)


def spread(keys, values, mask, qs, dos, stat, dq, s_ref, d_ref, p_ref, ds_ref):
    size = keys[0].shape[0]
    dk, dv = [0.0] * PACK, [0.0] * PACK

    def scores(h, at, to):
        s_ref[:size, to] = score(keys[h], qs[to], mask) - stat[h, 0:1, at]
        d_ref[:size, to] = dot(values[h], dos[to], NT) - stat[h, 1:2, at]

    def weights(h, at, to):
        p = jnp.exp2(s_ref[:size, to])
        p_ref[:size, to] = p.astype(BF16)
        ds_ref[:size, to] = (p * d_ref[:size, to]).astype(BF16)

    def mix(h, at, to):
        dk[h] = dk[h] + dot(ds_ref[:size, to], qs[to])
        dv[h] = dv[h] + dot(p_ref[:size, to], dos[to])
        dq[h, :, at] += dot(keys[h], ds_ref[:size, to], TN)

    stagger(scores, weights, mix)
    return [(x * SCALE).astype(BF16) for x in dk], [x.astype(BF16) for x in dv]


def lane(h):
    return slice(h * HEAD, (h + 1) * HEAD)


def chunk(near, which):
    return [near[:, which, :, lane(h)].reshape(KEYS, HEAD) for h in range(PACK)]


def near_fwd_body(bias, q_ref, near, stat, acc, qs, s_ref, p_ref):
    qs[...] = heads(q_ref)
    stat[:, 0:1] = jnp.full((PACK, 1, WIDE), MASKED, F32)
    stat[:, 1:2] = jnp.zeros((PACK, 1, WIDE), F32)
    acc[...] = jnp.zeros_like(acc)

    absorb(chunk(near, 0), chunk(near, 1), bias[...], qs, stat, acc, s_ref, p_ref)


def tail(far, which):
    return [far[:, which, :, lane(h)].reshape(TAIL, HEAD) for h in range(PACK)]


def far_body(
    flag, bias, q_ref, do_ref, far, stat_in, acc_in, o_ref, stat_out, dq, dfar, qs, dos, stat, acc, s_ref, d_ref, p_ref, ds_ref
):
    stat[...] = stat_in[...]
    acc[...] = acc_in[...]
    dq[...] = jnp.zeros_like(dq)

    @pl.when(flag[0] > 0)
    def _():
        qs[...] = heads(q_ref)
        dos[...] = heads(do_ref)
        absorb(tail(far, 0), tail(far, 1), bias[...], qs, stat, acc, s_ref, p_ref)

    for h in range(PACK):
        norm = stat[h, 1:2]
        out = (acc[h] * (1.0 / norm)).astype(BF16)
        stat_out[h, 0:1] = stat[h, 0:1] + jnp.log2(norm)
        for g in range(GROUP):
            at, to = lane(g), lane(h * GROUP + g)
            o_ref[:, to] = out[:, at].T
            prod = do_ref[:, to].T.astype(F32) * out[:, at].astype(F32)
            stat_out[h, 1:2, at] = jnp.sum(prod, axis=0, keepdims=True)

    @pl.when(flag[0] > 0)
    def _():
        dk, dv = spread(
            tail(far, 0), tail(far, 1), bias[...], qs, dos, stat_out, dq, s_ref, d_ref, p_ref, ds_ref
        )
        for h in range(PACK):
            dfar[:, 0, :, lane(h)] = dk[h].reshape(8, 16, HEAD)
            dfar[:, 1, :, lane(h)] = dv[h].reshape(8, 16, HEAD)

    @pl.when(flag[0] == 0)
    def _():
        dfar[...] = jnp.zeros_like(dfar)


def near_bwd_body(bias, q_ref, do_ref, near, stat, dq_in, dq_ref, dnear, qs, dos, dq, s_ref, d_ref, p_ref, ds_ref):
    qs[...] = heads(q_ref)
    dos[...] = heads(do_ref)
    dq[...] = dq_in[...]
    dk, dv = spread(chunk(near, 0), chunk(near, 1), bias[...], qs, dos, stat, dq, s_ref, d_ref, p_ref, ds_ref)
    for h in range(PACK):
        dnear[:, 0, :, lane(h)] = dk[h].reshape(8, ROWS, HEAD)
        dnear[:, 1, :, lane(h)] = dv[h].reshape(8, ROWS, HEAD)
    for h in range(PACK):
        for g in range(GROUP):
            dq_ref[:, lane(h * GROUP + g)] = (dq[h, :, lane(g)] * SCALE).astype(BF16).T


def shape(dims, dtype=BF16):
    return jax.ShapeDtypeStruct(dims, dtype)


STAT = shape((KV_HEADS, 2, WIDE), F32)
ACC = shape((KV_HEADS, HEAD, WIDE), F32)
TALL = shape((PACK * WIDE, HEAD))


def spec(a):
    if len(a.shape) == 2:
        return pl.BlockSpec((ROWS, PACK * WIDE), lambda k: (0, k))
    if len(a.shape) == 4:
        return pl.BlockSpec(a.shape[:3] + (PACK * HEAD,), lambda k: (0, 0, 0, k))
    return pl.BlockSpec((PACK,) + a.shape[1:], lambda k: (k, 0, 0))


def call(body, lead, args, outs, scratch, keys, products):
    size = keys * WIDE * KV_HEADS
    return pl.pallas_call(
        body,
        grid=(KV_HEADS // PACK,),
        in_specs=[pl.BlockSpec(memory_space=pltpu.SMEM) for a in lead[:-1]]
        + [pl.BlockSpec(lead[-1].shape, lambda k: (0, 0))]
        + [spec(a) for a in args],
        out_specs=[spec(a) for a in outs],
        out_shape=outs,
        scratch_shapes=[pltpu.VMEM(a.shape, a.dtype) for a in scratch],
        compiler_params=pltpu.CompilerParams(vmem_limit_bytes=VMEM),
        cost_estimate=pl.CostEstimate(
            flops=4 * products * HEAD * size, bytes_accessed=16 * 2**20, transcendentals=size
        ),
    )(*lead, *args)


ONE_STAT = shape((PACK, 2, WIDE), F32)
ONE_ACC = shape((PACK, HEAD, WIDE), F32)


def slabs(keys):
    wide = (keys, PACK * WIDE)
    return [shape(wide, F32), shape(wide, F32), shape(wide), shape(wide)]


def near_fwd(bias, q, near):
    scratch = [TALL, slabs(KEYS)[0], slabs(KEYS)[2]]
    return call(near_fwd_body, [bias], [q, near], [STAT, ACC], scratch, 1024, 2)


def far_both(flag, bias, q, grad, far, stat, acc):
    outs = [shape(q.shape), STAT, ACC, shape(far.shape)]
    scratch = [TALL, TALL, ONE_STAT, ONE_ACC, *slabs(TAIL)]
    return call(far_body, [flag, bias], [q, grad, far, stat, acc], outs, scratch, TAIL, 12)


def near_bwd(bias, q, grad, near, stat, dq):
    outs = [shape(q.shape), shape(near.shape)]
    scratch = [TALL, TALL, ONE_ACC, *slabs(KEYS)]
    args = [q, grad, near, stat, dq]
    return call(near_bwd_body, [bias], args, outs, scratch, 1024, 5)


def split(block):
    rows = block.shape[1] // 8
    return block.reshape(2, rows, 8, 8, HEAD).transpose(0, 1, 3, 2, 4).reshape(16 * rows, 8, HEAD)


def join(pieces):
    rows = pieces.shape[0] // 16
    return pieces.reshape(2, rows, 8, 8, HEAD).transpose(0, 1, 3, 2, 4).reshape(2, rows * 8, 1024)


def swap(pieces, axis):
    return lax.all_to_all(pieces, axis, split_axis=0, concat_axis=0, tiled=True)


def route(block, choose):
    pieces = swap(split(block), "dp").reshape(32, 8 * HEAD)
    pieces = jnp.dot(choose, pieces, preferred_element_type=F32).astype(BF16)
    return join(swap(pieces.reshape(32, 8, HEAD), "dp"))


def scatter_last(kv, z):
    half = lax.ppermute(kv[:, :64], "head", [(7, 3)])
    mine = jnp.where(z == 7, kv[:, 64:], half)
    send = jnp.where(z == 7, mine[:, :32], half[:, :32])
    quarter = lax.ppermute(send, "head", [(7, 5), (3, 1)])
    send = jnp.where(z % 4 == 3, mine[:, 32:48], quarter[:, :16])
    eighth = lax.ppermute(send, "head", [(7, 6), (5, 4), (3, 2), (1, 0)])
    return jnp.where(z % 2 == 0, eighth, jnp.where(z % 4 == 1, quarter[:, 16:], mine[:, 48:]))


def collect_last(piece):
    two = lax.ppermute(piece, "head", [(i, i + 1) for i in (0, 2, 4, 6)])
    two = jnp.concatenate([two, piece], axis=1)
    four = lax.ppermute(two, "head", [(1, 3), (5, 7)])
    four = jnp.concatenate([four, two], axis=1)
    eight = lax.ppermute(four, "head", [(3, 7)])
    return jnp.concatenate([eight, four], axis=1)


def per_device(queries, input_keys, input_values, output_gradient, doc_ids, spill_src, spill_len):
    rank, z = lax.axis_index("dp"), lax.axis_index("head")
    ids = jnp.arange(32, dtype=jnp.int32)
    kv = jnp.stack([input_keys, input_values])
    near = lax.all_gather(kv, "head", axis=0)

    wanted = (spill_src[:, None] == ids[None, :]).astype(BF16)
    piece = route(scatter_last(kv, z), wanted)
    near, piece = lax.optimization_barrier((near, piece))
    far = swap(jnp.broadcast_to(piece[None], (8, 2, 16, 1024)), "head")

    place = jnp.arange(1024, dtype=jnp.int32)
    row_at = z * ROWS + jnp.arange(ROWS, dtype=jnp.int32)
    row_docs = lax.dynamic_slice_in_dim(doc_ids, z * ROWS, ROWS)
    near_seen = (doc_ids[:, None] == row_docs[None, :]) & (place[:, None] <= row_at[None, :])
    far_seen = (place[:TAIL, None] >= TAIL - spill_len[rank]) & (row_docs[None, :] == 0)
    near_bias = jnp.where(near_seen, 0.0, MASKED).astype(F32)
    far_bias = jnp.where(far_seen, 0.0, MASKED).astype(F32)
    flag = (row_docs[:1] == 0).astype(jnp.int32)

    stat, acc = near_fwd(near_bias, queries, near)
    out, stat, dq, dfar = far_both(flag, far_bias, queries, output_gradient, far, stat, acc)
    parts = swap(dfar, "head")
    args = (near_bias, queries, output_gradient, near, stat, dq)
    dq, dnear = near_bwd(*args)
    dnear, parts = lax.optimization_barrier((dnear, parts))

    home = lax.psum_scatter(dnear, "head", scatter_dimension=0)
    piece = jnp.sum(parts.astype(F32), axis=0).astype(BF16)
    returned = collect_last(route(piece, wanted.T))
    totals = [
        (home[i].astype(F32) + jnp.where(z == 7, returned[i].astype(F32), 0.0)).astype(BF16) for i in range(2)
    ]
    return out, dq, *totals


def solution(mesh):
    rows = P(("dp", "head"), None)
    return jax.shard_map(
        per_device,
        mesh=mesh,
        in_specs=(rows, rows, rows, rows, P("dp"), P(), P()),
        out_specs=(rows, rows, rows, rows),
        check_vma=False,
    )
```

```python
import functools

import jax
import jax.numpy as jnp
from jax import lax
from jax.experimental import pallas as pl
from jax.experimental.pallas import tpu as pltpu
from jax.sharding import PartitionSpec as P

HEAD = 128
GROUP = 8
KV_HEADS = 8
ROWS = 128
WIDE = GROUP * ROWS
TAIL = 128
PAIR = 256
LOG2E = 1.4426950408889634
SCALE = HEAD**-0.5
MASKED = -1e30
F32 = jnp.float32
BF16 = jnp.bfloat16
NT = (((1,), (1,)), ((), ()))
TN = (((0,), (0,)), ((), ()))
KEYS = 1024
PACK = 2
VMEM = 60 * 2**20


def dot(a, b, dims=(((1,), (0,)), ((), ()))):
    return lax.dot_general(a, b, dims, preferred_element_type=F32)


def fold(x, op):
    return op(x.reshape(x.shape[0] // 8, 8, x.shape[1]), axis=0)


def heads(ref):
    return jnp.concatenate([ref[:, g * HEAD : (g + 1) * HEAD] for g in range(PACK * GROUP)], axis=0)


SLICES = [(at // WIDE, slice(at % WIDE, at % WIDE + PAIR), slice(at, at + PAIR)) for at in range(0, PACK * WIDE, PAIR)]


def stagger(*stages):
    for step in range(len(SLICES) + len(stages) - 1):
        for late, stage in enumerate(stages):
            if 0 <= step - late < len(SLICES):
                stage(*SLICES[step - late])


def score(keys, q2, mask):
    return dot(keys, q2, NT) * (SCALE * LOG2E) + jnp.concatenate([mask, mask], axis=1)


def absorb(keys, values, mask, qs, stat, acc, s_ref, p_ref):
    size = keys[0].shape[0]
    kept = {}

    def scores(h, at, to):
        s = score(keys[h], qs[to], mask)
        s_ref[:size, to] = s
        top = jnp.max(fold(s, jnp.max), axis=0, keepdims=True)
        kept[to.start] = jnp.maximum(stat[h, 0:1, at], top)

    def weights(h, at, to):
        high = kept[to.start]
        p = jnp.exp2(s_ref[:size, to] - high)
        p_ref[:size, to] = p.astype(BF16)
        alpha = jnp.exp2(stat[h, 0:1, at] - high)
        stat[h, 0:1, at] = high
        stat[h, 1:2, at] = stat[h, 1:2, at] * alpha + jnp.sum(fold(p, jnp.sum), axis=0, keepdims=True)
        kept[to.start] = alpha

    def mix(h, at, to):
        acc[h, :, at] = acc[h, :, at] * kept[to.start] + dot(values[h], p_ref[:size, to], TN)

    stagger(scores, weights, mix)


def spread(keys, values, mask, qs, dos, stat, dq, s_ref, d_ref, p_ref, ds_ref):
    size = keys[0].shape[0]
    dk, dv = [0.0] * PACK, [0.0] * PACK

    def scores(h, at, to):
        s_ref[:size, to] = score(keys[h], qs[to], mask) - stat[h, 0:1, at]
        d_ref[:size, to] = dot(values[h], dos[to], NT) - stat[h, 1:2, at]

    def weights(h, at, to):
        p = jnp.exp2(s_ref[:size, to])
        p_ref[:size, to] = p.astype(BF16)
        ds_ref[:size, to] = (p * d_ref[:size, to]).astype(BF16)

    def mix(h, at, to):
        dk[h] = dk[h] + dot(ds_ref[:size, to], qs[to])
        dv[h] = dv[h] + dot(p_ref[:size, to], dos[to])
        dq[h, :, at] += dot(keys[h], ds_ref[:size, to], TN)

    stagger(scores, weights, mix)
    return [(x * SCALE).astype(BF16) for x in dk], [x.astype(BF16) for x in dv]


def lane(h):
    return slice(h * HEAD, (h + 1) * HEAD)


def chunk(near, which):
    return [near[:, which, :, lane(h)].reshape(KEYS, HEAD) for h in range(PACK)]


def near_fwd_body(bias, q_ref, near, stat, acc, qs, s_ref, p_ref):
    qs[...] = heads(q_ref)
    stat[:, 0:1] = jnp.full((PACK, 1, WIDE), MASKED, F32)
    stat[:, 1:2] = jnp.zeros((PACK, 1, WIDE), F32)
    acc[...] = jnp.zeros_like(acc)

    absorb(chunk(near, 0), chunk(near, 1), bias[...], qs, stat, acc, s_ref, p_ref)


def tail(far, which):
    return [far[:, which, :, lane(h)].reshape(TAIL, HEAD) for h in range(PACK)]


def far_body(
    flag, bias, q_ref, do_ref, far, stat_in, acc_in, o_ref, stat_out, dq, dfar, qs, dos, stat, acc, s_ref, d_ref, p_ref, ds_ref
):
    stat[...] = stat_in[...]
    acc[...] = acc_in[...]
    dq[...] = jnp.zeros_like(dq)

    @pl.when(flag[0] > 0)
    def _():
        qs[...] = heads(q_ref)
        dos[...] = heads(do_ref)
        absorb(tail(far, 0), tail(far, 1), bias[...], qs, stat, acc, s_ref, p_ref)

    for h in range(PACK):
        norm = stat[h, 1:2]
        out = (acc[h] * (1.0 / norm)).astype(BF16)
        stat_out[h, 0:1] = stat[h, 0:1] + jnp.log2(norm)
        for g in range(GROUP):
            at, to = lane(g), lane(h * GROUP + g)
            o_ref[:, to] = out[:, at].T
            prod = do_ref[:, to].T.astype(F32) * out[:, at].astype(F32)
            stat_out[h, 1:2, at] = jnp.sum(prod, axis=0, keepdims=True)

    @pl.when(flag[0] > 0)
    def _():
        dk, dv = spread(
            tail(far, 0), tail(far, 1), bias[...], qs, dos, stat_out, dq, s_ref, d_ref, p_ref, ds_ref
        )
        for h in range(PACK):
            dfar[:, 0, :, lane(h)] = dk[h].reshape(8, 16, HEAD)
            dfar[:, 1, :, lane(h)] = dv[h].reshape(8, 16, HEAD)

    @pl.when(flag[0] == 0)
    def _():
        dfar[...] = jnp.zeros_like(dfar)


def near_bwd_body(bias, q_ref, do_ref, near, stat, dq_in, dq_ref, dnear, qs, dos, dq, s_ref, d_ref, p_ref, ds_ref):
    qs[...] = heads(q_ref)
    dos[...] = heads(do_ref)
    dq[...] = dq_in[...]
    dk, dv = spread(chunk(near, 0), chunk(near, 1), bias[...], qs, dos, stat, dq, s_ref, d_ref, p_ref, ds_ref)
    for h in range(PACK):
        dnear[:, 0, :, lane(h)] = dk[h].reshape(8, ROWS, HEAD)
        dnear[:, 1, :, lane(h)] = dv[h].reshape(8, ROWS, HEAD)
    for h in range(PACK):
        for g in range(GROUP):
            dq_ref[:, lane(h * GROUP + g)] = (dq[h, :, lane(g)] * SCALE).astype(BF16).T


def shape(dims, dtype=BF16):
    return jax.ShapeDtypeStruct(dims, dtype)


STAT = shape((KV_HEADS, 2, WIDE), F32)
ACC = shape((KV_HEADS, HEAD, WIDE), F32)
TALL = shape((PACK * WIDE, HEAD))


def spec(a):
    if len(a.shape) == 2:
        return pl.BlockSpec((ROWS, PACK * WIDE), lambda k: (0, k))
    if len(a.shape) == 4:
        return pl.BlockSpec(a.shape[:3] + (PACK * HEAD,), lambda k: (0, 0, 0, k))
    return pl.BlockSpec((PACK,) + a.shape[1:], lambda k: (k, 0, 0))


def call(body, lead, args, outs, scratch, keys, products):
    size = keys * WIDE * KV_HEADS
    return pl.pallas_call(
        body,
        grid=(KV_HEADS // PACK,),
        in_specs=[pl.BlockSpec(memory_space=pltpu.SMEM) for a in lead[:-1]]
        + [pl.BlockSpec(lead[-1].shape, lambda k: (0, 0))]
        + [spec(a) for a in args],
        out_specs=[spec(a) for a in outs],
        out_shape=outs,
        scratch_shapes=[pltpu.VMEM(a.shape, a.dtype) for a in scratch],
        compiler_params=pltpu.CompilerParams(vmem_limit_bytes=VMEM),
        cost_estimate=pl.CostEstimate(
            flops=4 * products * HEAD * size, bytes_accessed=16 * 2**20, transcendentals=size
        ),
    )(*lead, *args)


ONE_STAT = shape((PACK, 2, WIDE), F32)
ONE_ACC = shape((PACK, HEAD, WIDE), F32)


def slabs(keys):
    wide = (keys, PACK * WIDE)
    return [shape(wide, F32), shape(wide, F32), shape(wide), shape(wide)]


def near_fwd(bias, q, near):
    scratch = [TALL, slabs(KEYS)[0], slabs(KEYS)[2]]
    return call(near_fwd_body, [bias], [q, near], [STAT, ACC], scratch, 1024, 2)


def far_both(flag, bias, q, grad, far, stat, acc):
    outs = [shape(q.shape), STAT, ACC, shape(far.shape)]
    scratch = [TALL, TALL, ONE_STAT, ONE_ACC, *slabs(TAIL)]
    return call(far_body, [flag, bias], [q, grad, far, stat, acc], outs, scratch, TAIL, 12)


def near_bwd(bias, q, grad, near, stat, dq):
    outs = [shape(q.shape), shape(near.shape)]
    scratch = [TALL, TALL, ONE_ACC, *slabs(KEYS)]
    args = [q, grad, near, stat, dq]
    return call(near_bwd_body, [bias], args, outs, scratch, 1024, 5)


def split(block):
    rows = block.shape[1] // 8
    return block.reshape(2, rows, 8, 8, HEAD).transpose(0, 1, 3, 2, 4).reshape(16 * rows, 8, HEAD)


def join(pieces):
    rows = pieces.shape[0] // 16
    return pieces.reshape(2, rows, 8, 8, HEAD).transpose(0, 1, 3, 2, 4).reshape(2, rows * 8, 1024)


def swap(pieces, axis):
    return lax.all_to_all(pieces, axis, split_axis=0, concat_axis=0, tiled=True)


def route(block, choose):
    pieces = swap(split(block), "dp").reshape(32, 8 * HEAD)
    pieces = jnp.dot(choose, pieces, preferred_element_type=F32).astype(BF16)
    return join(swap(pieces.reshape(32, 8, HEAD), "dp"))


def scatter_last(kv, z):
    half = lax.ppermute(kv[:, :64], "head", [(7, 3)])
    mine = jnp.where(z == 7, kv[:, 64:], half)
    send = jnp.where(z == 7, mine[:, :32], half[:, :32])
    quarter = lax.ppermute(send, "head", [(7, 5), (3, 1)])
    send = jnp.where(z % 4 == 3, mine[:, 32:48], quarter[:, :16])
    eighth = lax.ppermute(send, "head", [(7, 6), (5, 4), (3, 2), (1, 0)])
    return jnp.where(z % 2 == 0, eighth, jnp.where(z % 4 == 1, quarter[:, 16:], mine[:, 48:]))


def collect_last(piece):
    two = lax.ppermute(piece, "head", [(i, i + 1) for i in (0, 2, 4, 6)])
    two = jnp.concatenate([two, piece], axis=1)
    four = lax.ppermute(two, "head", [(1, 3), (5, 7)])
    four = jnp.concatenate([four, two], axis=1)
    eight = lax.ppermute(four, "head", [(3, 7)])
    return jnp.concatenate([eight, four], axis=1)


def per_device(queries, input_keys, input_values, output_gradient, doc_ids, spill_src, spill_len):
    rank, z = lax.axis_index("dp"), lax.axis_index("head")
    ids = jnp.arange(32, dtype=jnp.int32)
    kv = lax.optimization_barrier(jnp.stack([input_keys, input_values]))
    near = lax.all_gather(kv, "head", axis=0)

    wanted = (spill_src[:, None] == ids[None, :]).astype(BF16)
    piece = route(scatter_last(kv, z), wanted)
    far = swap(jnp.broadcast_to(piece[None], (8, 2, 16, 1024)), "head")

    place = jnp.arange(1024, dtype=jnp.int32)
    row_at = z * ROWS + jnp.arange(ROWS, dtype=jnp.int32)
    row_docs = lax.dynamic_slice_in_dim(doc_ids, z * ROWS, ROWS)
    near_seen = (doc_ids[:, None] == row_docs[None, :]) & (place[:, None] <= row_at[None, :])
    far_seen = (place[:TAIL, None] >= TAIL - spill_len[rank]) & (row_docs[None, :] == 0)
    near_bias = jnp.where(near_seen, 0.0, MASKED).astype(F32)
    far_bias = jnp.where(far_seen, 0.0, MASKED).astype(F32)
    flag = (row_docs[:1] == 0).astype(jnp.int32)

    stat, acc = near_fwd(near_bias, queries, near)
    out, stat, dq, dfar = far_both(flag, far_bias, queries, output_gradient, far, stat, acc)
    parts = swap(dfar, "head")
    args = (near_bias, queries, output_gradient, near, stat, dq)
    dq, dnear = near_bwd(*args)
    dnear, parts = lax.optimization_barrier((dnear, parts))

    home = lax.psum_scatter(dnear, "head", scatter_dimension=0)
    piece = jnp.sum(parts.astype(F32), axis=0).astype(BF16)
    returned = collect_last(route(piece, wanted.T))
    totals = [
        (home[i].astype(F32) + jnp.where(z == 7, returned[i].astype(F32), 0.0)).astype(BF16) for i in range(2)
    ]
    return out, dq, *totals


def solution(mesh):
    rows = P(("dp", "head"), None)
    return jax.shard_map(
        per_device,
        mesh=mesh,
        in_specs=(rows, rows, rows, rows, P("dp"), P(), P()),
        out_specs=(rows, rows, rows, rows),
        check_vma=False,
    )
```

```python
import functools

import jax
import jax.numpy as jnp
from jax import lax
from jax.experimental import pallas as pl
from jax.experimental.pallas import tpu as pltpu
from jax.sharding import PartitionSpec as P

HEAD = 128
GROUP = 8
KV_HEADS = 8
ROWS = 128
WIDE = GROUP * ROWS
TAIL = 128
PAIR = 256
LOG2E = 1.4426950408889634
SCALE = HEAD**-0.5
MASKED = -1e30
F32 = jnp.float32
BF16 = jnp.bfloat16
NT = (((1,), (1,)), ((), ()))
TN = (((0,), (0,)), ((), ()))
KEYS = 1024
PACK = 2
VMEM = 60 * 2**20


def dot(a, b, dims=(((1,), (0,)), ((), ()))):
    return lax.dot_general(a, b, dims, preferred_element_type=F32)


def fold(x, op):
    return op(x.reshape(x.shape[0] // 8, 8, x.shape[1]), axis=0)


def heads(ref):
    return jnp.concatenate([ref[:, g * HEAD : (g + 1) * HEAD] for g in range(PACK * GROUP)], axis=0)


SLICES = [(at // WIDE, slice(at % WIDE, at % WIDE + PAIR), slice(at, at + PAIR)) for at in range(0, PACK * WIDE, PAIR)]


def stagger(*stages):
    for step in range(len(SLICES) + len(stages) - 1):
        for late, stage in enumerate(stages):
            if 0 <= step - late < len(SLICES):
                stage(*SLICES[step - late])


def score(keys, q2, mask):
    return dot(keys, q2, NT) * (SCALE * LOG2E) + jnp.concatenate([mask, mask], axis=1)


def absorb(keys, values, mask, qs, stat, acc, s_ref, p_ref):
    size = keys[0].shape[0]
    kept = {}

    def scores(h, at, to):
        s = score(keys[h], qs[to], mask)
        s_ref[:size, to] = s
        top = jnp.max(fold(s, jnp.max), axis=0, keepdims=True)
        kept[to.start] = jnp.maximum(stat[h, 0:1, at], top)

    def weights(h, at, to):
        high = kept[to.start]
        p = jnp.exp2(s_ref[:size, to] - high)
        p_ref[:size, to] = p.astype(BF16)
        alpha = jnp.exp2(stat[h, 0:1, at] - high)
        stat[h, 0:1, at] = high
        stat[h, 1:2, at] = stat[h, 1:2, at] * alpha + jnp.sum(fold(p, jnp.sum), axis=0, keepdims=True)
        kept[to.start] = alpha

    def mix(h, at, to):
        acc[h, :, at] = acc[h, :, at] * kept[to.start] + dot(values[h], p_ref[:size, to], TN)

    stagger(scores, weights, mix)


def spread(keys, values, mask, qs, dos, stat, dq, s_ref, d_ref, p_ref, ds_ref):
    size = keys[0].shape[0]
    dk, dv = [0.0] * PACK, [0.0] * PACK

    def scores(h, at, to):
        s_ref[:size, to] = score(keys[h], qs[to], mask) - stat[h, 0:1, at]
        d_ref[:size, to] = dot(values[h], dos[to], NT) - stat[h, 1:2, at]

    def weights(h, at, to):
        p = jnp.exp2(s_ref[:size, to])
        p_ref[:size, to] = p.astype(BF16)
        ds_ref[:size, to] = (p * d_ref[:size, to]).astype(BF16)

    def mix(h, at, to):
        dk[h] = dk[h] + dot(ds_ref[:size, to], qs[to])
        dv[h] = dv[h] + dot(p_ref[:size, to], dos[to])
        dq[h, :, at] += dot(keys[h], ds_ref[:size, to], TN)

    stagger(scores, weights, mix)
    return [(x * SCALE).astype(BF16) for x in dk], [x.astype(BF16) for x in dv]


def lane(h):
    return slice(h * HEAD, (h + 1) * HEAD)


def chunk(near, which):
    return [near[:, which, :, lane(h)].reshape(KEYS, HEAD) for h in range(PACK)]


def near_fwd_body(bias, q_ref, near, stat, acc, qs, s_ref, p_ref):
    qs[...] = heads(q_ref)
    stat[:, 0:1] = jnp.full((PACK, 1, WIDE), MASKED, F32)
    stat[:, 1:2] = jnp.zeros((PACK, 1, WIDE), F32)
    acc[...] = jnp.zeros_like(acc)

    absorb(chunk(near, 0), chunk(near, 1), bias[...], qs, stat, acc, s_ref, p_ref)


def tail(far, which):
    return [far[:, which, :, lane(h)].reshape(TAIL, HEAD) for h in range(PACK)]


def far_body(
    flag, bias, q_ref, do_ref, far, stat_in, acc_in, o_ref, stat_out, dq, dfar, qs, dos, stat, acc, s_ref, d_ref, p_ref, ds_ref
):
    stat[...] = stat_in[...]
    acc[...] = acc_in[...]
    dq[...] = jnp.zeros_like(dq)

    @pl.when(flag[0] > 0)
    def _():
        qs[...] = heads(q_ref)
        dos[...] = heads(do_ref)
        absorb(tail(far, 0), tail(far, 1), bias[...], qs, stat, acc, s_ref, p_ref)

    for h in range(PACK):
        norm = stat[h, 1:2]
        out = (acc[h] * (1.0 / norm)).astype(BF16)
        stat_out[h, 0:1] = stat[h, 0:1] + jnp.log2(norm)
        for g in range(GROUP):
            at, to = lane(g), lane(h * GROUP + g)
            o_ref[:, to] = out[:, at].T
            prod = do_ref[:, to].T.astype(F32) * out[:, at].astype(F32)
            stat_out[h, 1:2, at] = jnp.sum(prod, axis=0, keepdims=True)

    @pl.when(flag[0] > 0)
    def _():
        dk, dv = spread(
            tail(far, 0), tail(far, 1), bias[...], qs, dos, stat_out, dq, s_ref, d_ref, p_ref, ds_ref
        )
        for h in range(PACK):
            dfar[:, 0, :, lane(h)] = dk[h].reshape(8, 16, HEAD)
            dfar[:, 1, :, lane(h)] = dv[h].reshape(8, 16, HEAD)

    @pl.when(flag[0] == 0)
    def _():
        dfar[...] = jnp.zeros_like(dfar)


def near_bwd_body(bias, q_ref, do_ref, near, stat, dq_in, dq_ref, dnear, qs, dos, dq, s_ref, d_ref, p_ref, ds_ref):
    qs[...] = heads(q_ref)
    dos[...] = heads(do_ref)
    dq[...] = dq_in[...]
    dk, dv = spread(chunk(near, 0), chunk(near, 1), bias[...], qs, dos, stat, dq, s_ref, d_ref, p_ref, ds_ref)
    for h in range(PACK):
        dnear[:, 0, :, lane(h)] = dk[h].reshape(8, ROWS, HEAD)
        dnear[:, 1, :, lane(h)] = dv[h].reshape(8, ROWS, HEAD)
    for h in range(PACK):
        for g in range(GROUP):
            dq_ref[:, lane(h * GROUP + g)] = (dq[h, :, lane(g)] * SCALE).astype(BF16).T


def shape(dims, dtype=BF16):
    return jax.ShapeDtypeStruct(dims, dtype)


STAT = shape((KV_HEADS, 2, WIDE), F32)
ACC = shape((KV_HEADS, HEAD, WIDE), F32)
TALL = shape((PACK * WIDE, HEAD))


def spec(a):
    if len(a.shape) == 2:
        return pl.BlockSpec((ROWS, PACK * WIDE), lambda k: (0, k))
    if len(a.shape) == 4:
        return pl.BlockSpec(a.shape[:3] + (PACK * HEAD,), lambda k: (0, 0, 0, k))
    return pl.BlockSpec((PACK,) + a.shape[1:], lambda k: (k, 0, 0))


def call(body, lead, args, outs, scratch, keys, products):
    size = keys * WIDE * KV_HEADS
    return pl.pallas_call(
        body,
        grid=(KV_HEADS // PACK,),
        in_specs=[pl.BlockSpec(memory_space=pltpu.SMEM) for a in lead[:-1]]
        + [pl.BlockSpec(lead[-1].shape, lambda k: (0, 0))]
        + [spec(a) for a in args],
        out_specs=[spec(a) for a in outs],
        out_shape=outs,
        scratch_shapes=[pltpu.VMEM(a.shape, a.dtype) for a in scratch],
        compiler_params=pltpu.CompilerParams(vmem_limit_bytes=VMEM),
        cost_estimate=pl.CostEstimate(
            flops=4 * products * HEAD * size, bytes_accessed=16 * 2**20, transcendentals=size
        ),
    )(*lead, *args)


ONE_STAT = shape((PACK, 2, WIDE), F32)
ONE_ACC = shape((PACK, HEAD, WIDE), F32)


def slabs(keys):
    wide = (keys, PACK * WIDE)
    return [shape(wide, F32), shape(wide, F32), shape(wide), shape(wide)]


def near_fwd(bias, q, near):
    scratch = [TALL, slabs(KEYS)[0], slabs(KEYS)[2]]
    return call(near_fwd_body, [bias], [q, near], [STAT, ACC], scratch, 1024, 2)


def far_both(flag, bias, q, grad, far, stat, acc):
    outs = [shape(q.shape), STAT, ACC, shape(far.shape)]
    scratch = [TALL, TALL, ONE_STAT, ONE_ACC, *slabs(TAIL)]
    return call(far_body, [flag, bias], [q, grad, far, stat, acc], outs, scratch, TAIL, 12)


def near_bwd(bias, q, grad, near, stat, dq):
    outs = [shape(q.shape), shape(near.shape)]
    scratch = [TALL, TALL, ONE_ACC, *slabs(KEYS)]
    args = [q, grad, near, stat, dq]
    return call(near_bwd_body, [bias], args, outs, scratch, 1024, 5)


def split(block):
    rows = block.shape[1] // 8
    return block.reshape(2, rows, 8, 8, HEAD).transpose(0, 1, 3, 2, 4).reshape(16 * rows, 8, HEAD)


def join(pieces):
    rows = pieces.shape[0] // 16
    return pieces.reshape(2, rows, 8, 8, HEAD).transpose(0, 1, 3, 2, 4).reshape(2, rows * 8, 1024)


def swap(pieces, axis):
    return lax.all_to_all(pieces, axis, split_axis=0, concat_axis=0, tiled=True)


def route(block, choose):
    pieces = swap(split(block), "dp").reshape(32, 8 * HEAD)
    pieces = jnp.dot(choose, pieces, preferred_element_type=F32).astype(BF16)
    return join(swap(pieces.reshape(32, 8, HEAD), "dp"))


def scatter_last(kv, z):
    parts = [lax.ppermute(kv[:, 32 * i : 32 * i + 32], "head", [(7, 2 * i + 1)]) for i in range(3)]
    two = jnp.where(z == 7, kv[:, 96:], jnp.where(z == 1, parts[0], jnp.where(z == 3, parts[1], parts[2])))
    even = lax.ppermute(two[:, :16], "head", [(i + 1, i) for i in (0, 2, 4, 6)])
    return jnp.where(z % 2 == 0, even, two[:, 16:])


def collect_last(piece):
    even = lax.ppermute(piece, "head", [(i, i + 1) for i in (0, 2, 4, 6)])
    two = jnp.concatenate([even, piece], axis=1)
    parts = [lax.ppermute(two, "head", [(i, 7)]) for i in (1, 3, 5)]
    return jnp.concatenate([*parts, two], axis=1)


def per_device(queries, input_keys, input_values, output_gradient, doc_ids, spill_src, spill_len):
    rank, z = lax.axis_index("dp"), lax.axis_index("head")
    ids = jnp.arange(32, dtype=jnp.int32)
    kv = lax.optimization_barrier(jnp.stack([input_keys, input_values]))
    near = lax.all_gather(kv, "head", axis=0)

    wanted = (spill_src[:, None] == ids[None, :]).astype(BF16)
    piece = route(scatter_last(kv, z), wanted)
    far = swap(jnp.broadcast_to(piece[None], (8, 2, 16, 1024)), "head")

    place = jnp.arange(1024, dtype=jnp.int32)
    row_at = z * ROWS + jnp.arange(ROWS, dtype=jnp.int32)
    row_docs = lax.dynamic_slice_in_dim(doc_ids, z * ROWS, ROWS)
    near_seen = (doc_ids[:, None] == row_docs[None, :]) & (place[:, None] <= row_at[None, :])
    far_seen = (place[:TAIL, None] >= TAIL - spill_len[rank]) & (row_docs[None, :] == 0)
    near_bias = jnp.where(near_seen, 0.0, MASKED).astype(F32)
    far_bias = jnp.where(far_seen, 0.0, MASKED).astype(F32)
    flag = (row_docs[:1] == 0).astype(jnp.int32)

    stat, acc = near_fwd(near_bias, queries, near)
    out, stat, dq, dfar = far_both(flag, far_bias, queries, output_gradient, far, stat, acc)
    parts = swap(dfar, "head")
    args = (near_bias, queries, output_gradient, near, stat, dq)
    dq, dnear = near_bwd(*args)
    dnear, parts = lax.optimization_barrier((dnear, parts))

    home = lax.psum_scatter(dnear, "head", scatter_dimension=0)
    piece = jnp.sum(parts.astype(F32), axis=0).astype(BF16)
    returned = collect_last(route(piece, wanted.T))
    totals = [
        (home[i].astype(F32) + jnp.where(z == 7, returned[i].astype(F32), 0.0)).astype(BF16) for i in range(2)
    ]
    return out, dq, *totals


def solution(mesh):
    rows = P(("dp", "head"), None)
    return jax.shard_map(
        per_device,
        mesh=mesh,
        in_specs=(rows, rows, rows, rows, P("dp"), P(), P()),
        out_specs=(rows, rows, rows, rows),
        check_vma=False,
    )
```
